32 devices in a mesh: pipe: 4 (over z), tensor: 8 (over y, x, core).
Axes of the slice: x: 2, y: 2, z: 4, core: 2. Of those that a mesh axis runs over, the one named last changes fastest.
Arguments:
- tokens: bfloat16 [8, 128, 4096], P(None, 'tensor'), may hold values from -60 to 60
- norm_gain: float32 [4, 4096], P('pipe'), may hold values from 0.25 to 1.75
- gate_weight: bfloat16 [4, 4096, 14336], P('pipe', None, 'tensor'), may hold values from -0.09375 to 0.09375
- up_weight: bfloat16 [4, 4096, 14336], P('pipe', None, 'tensor'), may hold values from -0.09375 to 0.09375
- down_weight: bfloat16 [4, 14336, 4096], P('pipe', 'tensor'), may hold values from -0.046875 to 0.046875
Outputs:
- states: bfloat16 [4, 8, 128, 4096], P('pipe', None, 'tensor')
The draws below stay inside these ranges and needn't reach their ends.
All inputs are finite; a program needn't handle non-finite values.
Results may differ from the reference program's by a relative error of at most 0.019.
Values may be sent and summed in bfloat16 or wider, within the bound.
No kernel may reach another device: no remote copies, remote signals or barrier semaphores. Data moves between devices by JAX's collectives and lax.ppermute only.
A program may use at most 128 MiB of HBM per device.

```python
import math
import jax
import jax.numpy as jnp
from jax import lax

D = 4096
FF = 14336
ROWS = 128
MB = 8
LAYERS = 4


def draw_tokens(key, part):
    key = jax.random.fold_in(key, 11)
    key_rows, key_cols, key_base = jax.random.split(key, 3)
    low = math.log(0.3)
    high = math.log(3.0)
    row_scale = jnp.exp(jax.random.uniform(key_rows, (MB, ROWS, 1), jnp.float32, low, high))
    col_scale = jnp.exp(jax.random.uniform(key_cols, (1, 1, D), jnp.float32, low, high))
    base = jnp.clip(jax.random.normal(key_base, (MB, ROWS, D), jnp.float32), -6.0, 6.0)
    return (base * row_scale * col_scale).astype(jnp.bfloat16)


def block_scale(rng, extent, pieces, low, top_value):
    loudness = 1.0
    for dim, parts in pieces:
        heights = jax.random.uniform(jax.random.fold_in(jax.random.fold_in(rng, 6), dim), (parts,), jnp.float32, low / len(pieces), top_value / len(pieces))
        loudness = loudness * jnp.repeat(jnp.exp(heights), extent[dim] // parts).reshape((-1,) + (1,) * (len(extent) - 1 - dim))
    return loudness


def normal_values(key, extent, width, bound, pieces=(), dtype=jnp.bfloat16):
    values = jax.random.normal(key, extent, jnp.float32) * width
    if len(pieces) > 0:
        values = block_scale(key, extent, pieces, -0.22, 0.18) * values
    return jnp.clip(values, min=-bound, max=bound).astype(dtype)


def setup_inputs(seed: int = 0) -> dict:
    keys = jax.random.split(jax.random.key(seed), 6)
    return {
        "tokens": draw_tokens(jax.random.fold_in(keys[5], 71), 0),
        "norm_gain": jnp.clip(1.0 + 0.15 * jax.random.normal(keys[1], (LAYERS, D), jnp.float32), 0.25, 1.75),
        "gate_weight": normal_values(keys[2], (LAYERS, D, FF), D ** -0.5, 0.09375, ((0, 4), (2, 8))),
        "up_weight": normal_values(keys[3], (LAYERS, D, FF), D ** -0.5, 0.09375, ((0, 4), (2, 8))),
        "down_weight": normal_values(keys[4], (LAYERS, FF, D), FF ** -0.5, 0.046875, ((0, 4), (1, 8))),
    }


def normalize(row_block, scale_gain):
    values = row_block.astype(jnp.float32)
    inv_rms = jax.lax.rsqrt(lax.optimization_barrier(jnp.mean(values * values, axis=-1, keepdims=True)) + 1e-05)
    return (values * inv_rms * scale_gain.astype(jnp.float32)).astype(jnp.bfloat16)

def reference(tokens, norm_gain, gate_weight, up_weight, down_weight):
    residual_rows = tokens.reshape(MB * ROWS, D)
    collected = []
    for layer_idx in range(LAYERS):
        normed = normalize(residual_rows, norm_gain[layer_idx])
        gate_out = jnp.dot(normed, gate_weight[layer_idx], preferred_element_type=jnp.float32)
        up_out = jnp.dot(normed, up_weight[layer_idx], preferred_element_type=jnp.float32)
        hidden = (jax.nn.silu(gate_out) * up_out).astype(jnp.bfloat16)
        branch = jnp.dot(hidden, down_weight[layer_idx], preferred_element_type=jnp.float32)
        residual_rows = (residual_rows.astype(jnp.float32) + branch).astype(jnp.bfloat16)
        collected.append(residual_rows.reshape(MB, ROWS, D))
    return jnp.stack(collected)
```

```python
import jax
import jax.numpy as jnp
from jax import lax
from jax.experimental import pallas as pl
from jax.experimental.pallas import tpu as pltpu
from jax.sharding import PartitionSpec as P

IN_FLIGHT = 2
BLOCK_ROWS = 16

VMEM = pl.BlockSpec(memory_space=pltpu.VMEM)
SMEM = pl.BlockSpec(memory_space=pltpu.SMEM)
ANY = pl.BlockSpec(memory_space=pl.ANY)


def call(kernel, outs, ins, specs, out_specs=None, scratch=(), limit=4, name=None, cost=None, aliases=None):
    ins = [pltpu.with_memory_space_constraint(x, pltpu.VMEM) if spec is VMEM else x for x, spec in zip(ins, specs)]
    return pl.pallas_call(
        kernel,
        out_shape=outs,
        in_specs=specs,
        out_specs=out_specs or [VMEM] * len(outs),
        scratch_shapes=list(scratch),
        compiler_params=pltpu.CompilerParams(vmem_limit_bytes=limit * 2**20),
        cost_estimate=cost,
        input_output_aliases=aliases or {},
        name=name,
    )(*ins)


def after(value, behind):
    return lax.optimization_barrier((value, behind))[0]


def after_all(values, behind):
    return list(lax.optimization_barrier((*values, behind))[:-1])


def array(shape):
    return pltpu.VMEM(shape, jnp.bfloat16)


def chunks(extent, most):
    step = max((c for c in range(128, most + 1, 128) if extent % c == 0), default=extent)
    return [slice(at, at + step) for at in range(0, extent, step)]


def enter_kernel(section, token_ref, arrived_ref, gain_ref, current_ref, normed_ref):
    current = jnp.where(section[0] == 0, token_ref[...], arrived_ref[...])
    current_ref[...] = current
    values = current.astype(jnp.float32)
    inv_rms = lax.rsqrt(jnp.mean(values * values, axis=-1, keepdims=True) + 1e-05)
    normed_ref[...] = (values * inv_rms * gain_ref[...]).astype(jnp.bfloat16)


def enter(section, token_rows, arrived, gain):
    outs = [array(arrived.shape)] * 2
    return call(enter_kernel, outs, (section, token_rows, arrived, gain), [SMEM, VMEM, VMEM, VMEM], name="enter")


def for_stored(slot, sections, blocks, section, leaving_ref, states_ref, sem, act):
    for number in range(sections):
        if 0 <= slot - IN_FLIGHT * number < blocks:

            @pl.when(section[0] == number)
            def _():
                act(pltpu.make_async_copy(leaving_ref, states_ref.at[slot - IN_FLIGHT * number], sem))


def compute(parts, gate_ref, up_ref, down_ref, keep_ref, give_ref, rows_ref, hidden_ref):
    at = 0
    for part in parts:
        rows_ref[at : at + part.shape[0]] = part[...]
        at += part.shape[0]
    for columns in chunks(gate_ref.shape[1], 256):
        gate = jnp.dot(rows_ref[...], gate_ref[:, columns], preferred_element_type=jnp.float32)
        up = jnp.dot(rows_ref[...], up_ref[:, columns], preferred_element_type=jnp.float32)
        hidden_ref[:, columns] = (gate / (1.0 + jnp.exp(-gate)) * up).astype(jnp.bfloat16)
    half = keep_ref.shape[0]
    for columns in chunks(down_ref.shape[1], 512):
        branch = jnp.dot(hidden_ref[...], down_ref[:, columns], preferred_element_type=jnp.float32)
        keep_ref[:, columns] = branch[:half].astype(jnp.bfloat16)
        give_ref[:, columns] = branch[half:].astype(jnp.bfloat16)


def feed_forward(parts, weights, sections, states_shape, section, leaving, states, touched):
    units, depth = weights[2].shape
    rows = sum(part.shape[0] for part in parts)
    outs = [array((rows // 2, depth))] * 2
    scratch = [pltpu.VMEM((rows, depth), jnp.bfloat16), pltpu.VMEM((rows, units), jnp.bfloat16)]
    cost = pl.CostEstimate(flops=6 * rows * depth * units, bytes_accessed=4 * rows * depth, transcendentals=rows * units)
    ins = [*parts, *weights]
    if leaving is None:
        if touched is not None:
            ins.append(touched)

        def kernel(*refs):
            compute(refs[: len(parts)], *refs[len(parts) : len(parts) + 3], *refs[-4:])

        return *call(
            kernel, outs, ins, [VMEM] * len(ins), scratch=scratch, name="feed_forward", cost=cost
        ), None

    stored_slot, leaving = leaving
    ins = [section, leaving, *ins]
    specs = [SMEM] + [VMEM] * (len(ins) - 1)
    aliases = {}
    if states is not None:
        aliases = {len(ins): len(outs)}
        ins.append(states)
        specs.append(ANY)

    def kernel(section, leaving_ref, *refs):
        keep_ref, give_ref, states_ref, rows_ref, hidden_ref, sem = refs[-6:]
        gate_ref, up_ref, down_ref = refs[len(parts) : len(parts) + 3]
        stored = (stored_slot, sections, states_shape[0], section, leaving_ref, states_ref, sem)
        for_stored(*stored, lambda copy: copy.start())
        compute(refs[: len(parts)], gate_ref, up_ref, down_ref, keep_ref, give_ref, rows_ref, hidden_ref)
        for_stored(*stored, lambda copy: copy.wait())

    return call(
        kernel, outs + [jax.ShapeDtypeStruct(states_shape, jnp.bfloat16)], ins, specs, [VMEM, VMEM, ANY],
        scratch + [pltpu.SemaphoreType.DMA], name="feed_forward", cost=cost, aliases=aliases,
    )


def touch_kernel(*refs):
    *weight_refs, out_ref = refs
    out_ref[...] = sum(ref[: out_ref.shape[0], : out_ref.shape[1]] for ref in weight_refs)


def touch(weights):
    return call(touch_kernel, [array((16, 128))], weights, [VMEM] * len(weights), name="touch")[0]


def store(slot, sections, section, leaving, states):
    def kernel(section, leaving_ref, _, states_ref, sem):
        stored = (slot, sections, states_ref.shape[0], section, leaving_ref, states_ref, sem)
        for_stored(*stored, lambda copy: copy.start())
        for_stored(*stored, lambda copy: copy.wait())

    return call(
        kernel, [jax.ShapeDtypeStruct(states.shape, states.dtype)], (section, leaving, states), [SMEM, VMEM, ANY],
        [ANY], [pltpu.SemaphoreType.DMA], name="store", aliases={2: 0},
    )[0]


def sums_kernel(keep_ref, got_ref, *out_refs):
    rows = out_refs[0].shape[0]
    for at, out_ref in enumerate(out_refs, 1):
        here = slice(at * rows, (at + 1) * rows)
        out_ref[...] = (keep_ref[here].astype(jnp.float32) + got_ref[here].astype(jnp.float32)).astype(jnp.bfloat16)


def chip_sums(keep, got, rows):
    count = keep.shape[0] // rows
    outs = [array((rows, keep.shape[1]))] * (count - 1)
    return call(sums_kernel, outs, (keep, got), [VMEM, VMEM], name="chip_sums")


def leave_kernel(current_ref, keep_ref, got_ref, *refs):
    *brought_refs, out_ref = refs
    here = slice(0, out_ref.shape[0])
    branch = keep_ref[here].astype(jnp.float32) + got_ref[here].astype(jnp.float32)
    for brought_ref in brought_refs:
        branch = branch + brought_ref[...].astype(jnp.float32)
    out_ref[...] = (current_ref[...].astype(jnp.float32) + branch).astype(jnp.bfloat16)


def leave(current, keep, got, brought):
    ins = (current, keep, got, *brought)
    return call(leave_kernel, [array(current.shape)], ins, [VMEM] * len(ins), name="leave")[0]


def local(tokens, norm_gain, gate_weight, up_weight, down_weight):
    batches, batch_rows, depth = tokens.shape
    joined = max(1, BLOCK_ROWS // batch_rows)
    blocks, rows = batches // joined, batch_rows * joined
    tokens = tokens.reshape(blocks, rows, depth)
    count = lax.axis_size("tensor")
    sections = lax.axis_size("pipe")
    onward = [(i, i + 1) for i in range(sections - 1)]
    section = lax.axis_index("pipe").astype(jnp.int32)[None]
    weights = [gate_weight[0], up_weight[0], down_weight[0]]

    def exchange(value, distance):
        return lax.ppermute(value, "tensor", [(i, i ^ distance) for i in range(count)])

    slots = blocks + IN_FLIGHT * (sections - 1)
    nothing = jnp.zeros(tokens.shape[1:], jnp.bfloat16)
    inside, adding, arrived, left = {}, {}, {}, {}
    states, behind = None, nothing

    def come(slot, behind):
        token_rows = after(tokens[min(slot, blocks - 1)], behind)
        current, normed = enter(section, token_rows, arrived.pop(slot, nothing), norm_gain)
        inside[slot] = current, normed, [exchange(normed, chip) for chip in range(2, count, 2)]
        return normed

    def pair_up(slot, behind):
        current, normed, others = inside[slot]
        if behind is not None:
            others = after_all(others, behind)
        mine = [normed] + others
        inside[slot] = current, mine + [exchange(part, 1) for part in mine]

    def multiply(slot, behind, states, touched=None):
        current, parts = inside.pop(slot)
        parts[0] = after(parts[0], behind)
        leaving = (slot - IN_FLIGHT, left.pop(slot - IN_FLIGHT)) if slot >= IN_FLIGHT else None
        keep, give, states = feed_forward(
            parts, weights, sections, tokens.shape, section, leaving, states, touched
        )
        adding[slot] = [current, keep, give]
        return keep, states

    def send(slot, behind):
        _, keep, give = adding[slot]
        adding[slot][2] = got = exchange(give if behind is None else after(give, behind), 1)
        sums = chip_sums(keep, got, rows)
        adding[slot].append([exchange(part, chip) for part, chip in zip(sums, range(2, count, 2))])
        return sums[0]

    def go(slot, behind):
        current, *rest = adding.pop(slot)
        left[slot] = leave(after(current, behind), *rest)
        if slot + IN_FLIGHT < slots:
            arrived[slot + IN_FLIGHT] = lax.ppermute(left[slot], "pipe", onward)
        return left[slot]

    behind = come(0, nothing)
    touched = touch(after_all(weights, behind))
    pair_up(0, touched)
    behind = come(1, behind)
    for slot in range(0, slots, 2):
        paired, more = slot + 1 < slots, slot + 2 < slots
        behind, states = multiply(slot, behind, states, touched if slot == 0 else None)
        others = inside[slot + 1][2] if paired else None
        if paired:
            pair_up(slot + 1, behind)
        behind = send(slot, others)
        if paired:
            behind, states = multiply(slot + 1, behind, states)
        behind = go(slot, behind)
        if paired:
            behind = send(slot + 1, behind)
        if more:
            behind = come(slot + 2, behind)
        if paired:
            behind = go(slot + 1, behind)
        if more:
            pair_up(slot + 2, behind)
        if slot + 3 < slots:
            behind = come(slot + 3, behind)
    for slot, leaving in left.items():
        states = store(slot, sections, section, leaving, states)
    return states.reshape(1, batches, batch_rows, depth)


def solution(mesh):
    in_specs = (
        P(None, "tensor", None),
        P("pipe", None),
        P("pipe", None, "tensor"),
        P("pipe", None, "tensor"),
        P("pipe", "tensor", None),
    )
    out_specs = P("pipe", None, "tensor", None)
    return jax.shard_map(local, mesh=mesh, in_specs=in_specs, out_specs=out_specs, check_vma=False)
```

```python
import jax
import jax.numpy as jnp
from jax import lax
from jax.experimental import pallas as pl
from jax.experimental.pallas import tpu as pltpu
from jax.sharding import PartitionSpec as P

IN_FLIGHT = 2
FIRST_COST = 6_000_000_000
BLOCK_ROWS = 16

VMEM = pl.BlockSpec(memory_space=pltpu.VMEM)
SMEM = pl.BlockSpec(memory_space=pltpu.SMEM)
ANY = pl.BlockSpec(memory_space=pl.ANY)


def call(kernel, outs, ins, specs, out_specs=None, scratch=(), limit=4, name=None, cost=None, aliases=None):
    ins = [pltpu.with_memory_space_constraint(x, pltpu.VMEM) if spec is VMEM else x for x, spec in zip(ins, specs)]
    return pl.pallas_call(
        kernel,
        out_shape=outs,
        in_specs=specs,
        out_specs=out_specs or [VMEM] * len(outs),
        scratch_shapes=list(scratch),
        compiler_params=pltpu.CompilerParams(vmem_limit_bytes=limit * 2**20),
        cost_estimate=cost,
        input_output_aliases=aliases or {},
        name=name,
    )(*ins)


def after(value, behind):
    return lax.optimization_barrier((value, behind))[0]


def after_all(values, behind):
    return list(lax.optimization_barrier((*values, behind))[:-1])


def array(shape):
    return pltpu.VMEM(shape, jnp.bfloat16)


def chunks(extent, most):
    step = max((c for c in range(128, most + 1, 128) if extent % c == 0), default=extent)
    return [slice(at, at + step) for at in range(0, extent, step)]


def enter_kernel(section, token_ref, arrived_ref, gain_ref, current_ref, normed_ref):
    current = jnp.where(section[0] == 0, token_ref[...], arrived_ref[...])
    current_ref[...] = current
    values = current.astype(jnp.float32)
    inv_rms = lax.rsqrt(jnp.mean(values * values, axis=-1, keepdims=True) + 1e-05)
    normed_ref[...] = (values * inv_rms * gain_ref[...]).astype(jnp.bfloat16)


def enter(section, token_rows, arrived, gain, cost=None):
    outs = [array(arrived.shape)] * 2
    return call(enter_kernel, outs, (section, token_rows, arrived, gain), [SMEM, VMEM, VMEM, VMEM], name="enter", cost=cost)


def for_stored(slot, sections, blocks, section, leaving_ref, states_ref, sem, act):
    for number in range(sections):
        if 0 <= slot - IN_FLIGHT * number < blocks:

            @pl.when(section[0] == number)
            def _():
                act(pltpu.make_async_copy(leaving_ref, states_ref.at[slot - IN_FLIGHT * number], sem))


def compute(parts, gate_ref, up_ref, down_ref, keep_ref, give_ref, rows_ref, hidden_ref):
    at = 0
    for part in parts:
        rows_ref[at : at + part.shape[0]] = part[...]
        at += part.shape[0]
    for columns in chunks(gate_ref.shape[1], 896):
        gate = jnp.dot(rows_ref[...], gate_ref[:, columns], preferred_element_type=jnp.float32)
        up = jnp.dot(rows_ref[...], up_ref[:, columns], preferred_element_type=jnp.float32)
        hidden_ref[:, columns] = (gate / (1.0 + jnp.exp(-gate)) * up).astype(jnp.bfloat16)
    half = keep_ref.shape[0]
    for columns in chunks(down_ref.shape[1], 1024):
        branch = jnp.dot(hidden_ref[...], down_ref[:, columns], preferred_element_type=jnp.float32)
        keep_ref[:, columns] = branch[:half].astype(jnp.bfloat16)
        give_ref[:, columns] = branch[half:].astype(jnp.bfloat16)


def feed_forward(parts, weights, sections, states_shape, section, leaving, states, touched):
    units, depth = weights[2].shape
    rows = sum(part.shape[0] for part in parts)
    outs = [array((rows // 2, depth))] * 2
    scratch = [pltpu.VMEM((rows, depth), jnp.bfloat16), pltpu.VMEM((rows, units), jnp.bfloat16)]
    cost = pl.CostEstimate(flops=6 * rows * depth * units, bytes_accessed=4 * rows * depth, transcendentals=rows * units)
    ins = [*parts, *weights]
    if leaving is None:
        if touched is not None:
            ins.append(touched)

        def kernel(*refs):
            compute(refs[: len(parts)], *refs[len(parts) : len(parts) + 3], *refs[-4:])

        return *call(
            kernel, outs, ins, [VMEM] * len(ins), scratch=scratch, name="feed_forward", cost=cost
        ), None

    stored_slot, leaving = leaving
    ins = [section, leaving, *ins]
    specs = [SMEM] + [VMEM] * (len(ins) - 1)
    aliases = {}
    if states is not None:
        aliases = {len(ins): len(outs)}
        ins.append(states)
        specs.append(ANY)

    def kernel(section, leaving_ref, *refs):
        keep_ref, give_ref, states_ref, rows_ref, hidden_ref, sem = refs[-6:]
        gate_ref, up_ref, down_ref = refs[len(parts) : len(parts) + 3]
        stored = (stored_slot, sections, states_shape[0], section, leaving_ref, states_ref, sem)
        for_stored(*stored, lambda copy: copy.start())
        compute(refs[: len(parts)], gate_ref, up_ref, down_ref, keep_ref, give_ref, rows_ref, hidden_ref)
        for_stored(*stored, lambda copy: copy.wait())

    return call(
        kernel, outs + [jax.ShapeDtypeStruct(states_shape, jnp.bfloat16)], ins, specs, [VMEM, VMEM, ANY],
        scratch + [pltpu.SemaphoreType.DMA], name="feed_forward", cost=cost, aliases=aliases,
    )


def touch_kernel(*refs):
    *weight_refs, out_ref = refs
    out_ref[...] = sum(ref[: out_ref.shape[0], : out_ref.shape[1]] for ref in weight_refs)


def touch(weights):
    return call(touch_kernel, [array((16, 128))], weights, [VMEM] * len(weights), name="touch")[0]


def store(slot, sections, section, leaving, states):
    def kernel(section, leaving_ref, _, states_ref, sem):
        stored = (slot, sections, states_ref.shape[0], section, leaving_ref, states_ref, sem)
        for_stored(*stored, lambda copy: copy.start())
        for_stored(*stored, lambda copy: copy.wait())

    return call(
        kernel, [jax.ShapeDtypeStruct(states.shape, states.dtype)], (section, leaving, states), [SMEM, VMEM, ANY],
        [ANY], [pltpu.SemaphoreType.DMA], name="store", aliases={2: 0},
    )[0]


def sums_kernel(keep_ref, got_ref, *out_refs):
    rows = out_refs[0].shape[0]
    for at, out_ref in enumerate(out_refs, 1):
        here = slice(at * rows, (at + 1) * rows)
        out_ref[...] = (keep_ref[here].astype(jnp.float32) + got_ref[here].astype(jnp.float32)).astype(jnp.bfloat16)


def chip_sums(keep, got, rows):
    count = keep.shape[0] // rows
    outs = [array((rows, keep.shape[1]))] * (count - 1)
    return call(sums_kernel, outs, (keep, got), [VMEM, VMEM], name="chip_sums")


def leave_kernel(current_ref, keep_ref, got_ref, *refs):
    *brought_refs, out_ref = refs
    here = slice(0, out_ref.shape[0])
    branch = keep_ref[here].astype(jnp.float32) + got_ref[here].astype(jnp.float32)
    for brought_ref in brought_refs:
        branch = branch + brought_ref[...].astype(jnp.float32)
    out_ref[...] = (current_ref[...].astype(jnp.float32) + branch).astype(jnp.bfloat16)


def leave(current, keep, got, brought):
    ins = (current, keep, got, *brought)
    return call(leave_kernel, [array(current.shape)], ins, [VMEM] * len(ins), name="leave")[0]


def local(tokens, norm_gain, gate_weight, up_weight, down_weight):
    batches, batch_rows, depth = tokens.shape
    joined = max(1, BLOCK_ROWS // batch_rows)
    blocks, rows = batches // joined, batch_rows * joined
    tokens = tokens.reshape(blocks, rows, depth)
    count = lax.axis_size("tensor")
    sections = lax.axis_size("pipe")
    onward = [(i, i + 1) for i in range(sections - 1)]
    section = lax.axis_index("pipe").astype(jnp.int32)[None]
    weights = [gate_weight[0], up_weight[0], down_weight[0]]

    def exchange(value, distance):
        return lax.ppermute(value, "tensor", [(i, i ^ distance) for i in range(count)])

    slots = blocks + IN_FLIGHT * (sections - 1)
    nothing = jnp.zeros(tokens.shape[1:], jnp.bfloat16)
    inside, adding, arrived, left = {}, {}, {}, {}
    states, behind = None, nothing

    def come(slot, behind):
        token_rows = after(tokens[min(slot, blocks - 1)], behind)
        cost = pl.CostEstimate(flops=FIRST_COST, bytes_accessed=0, transcendentals=0) if slot == 0 else None
        current, normed = enter(section, token_rows, arrived.pop(slot, nothing), norm_gain, cost)
        inside[slot] = current, normed, [exchange(normed, chip) for chip in range(2, count, 2)]
        return normed

    def pair_up(slot, behind):
        current, normed, others = inside[slot]
        if behind is not None:
            others = after_all(others, behind)
        mine = [normed] + others
        inside[slot] = current, mine + [exchange(part, 1) for part in mine]

    def multiply(slot, behind, states, touched=None):
        current, parts = inside.pop(slot)
        parts[0] = after(parts[0], behind)
        leaving = (slot - IN_FLIGHT, left.pop(slot - IN_FLIGHT)) if slot >= IN_FLIGHT else None
        keep, give, states = feed_forward(
            parts, weights, sections, tokens.shape, section, leaving, states, touched
        )
        adding[slot] = [current, keep, give]
        return keep, states

    def send(slot, behind):
        _, keep, give = adding[slot]
        adding[slot][2] = got = exchange(give if behind is None else after(give, behind), 1)
        sums = chip_sums(keep, got, rows)
        adding[slot].append([exchange(part, chip) for part, chip in zip(sums, range(2, count, 2))])
        return sums[0]

    def go(slot, behind):
        current, *rest = adding.pop(slot)
        left[slot] = leave(after(current, behind), *rest)
        if slot + IN_FLIGHT < slots:
            arrived[slot + IN_FLIGHT] = lax.ppermute(left[slot], "pipe", onward)
        return left[slot]

    behind = come(0, nothing)
    touched = touch(after_all(weights, behind))
    pair_up(0, touched)
    behind = come(1, behind)
    for slot in range(0, slots, 2):
        paired, more = slot + 1 < slots, slot + 2 < slots
        behind, states = multiply(slot, behind, states, touched if slot == 0 else None)
        others = inside[slot + 1][2] if paired else None
        if paired:
            pair_up(slot + 1, behind)
        behind = send(slot, others)
        if paired:
            behind, states = multiply(slot + 1, behind, states)
        behind = go(slot, behind)
        if paired:
            behind = send(slot + 1, behind)
        if more:
            behind = come(slot + 2, behind)
        if paired:
            behind = go(slot + 1, behind)
        if more:
            pair_up(slot + 2, behind)
        if slot + 3 < slots:
            behind = come(slot + 3, behind)
    for slot, leaving in left.items():
        states = store(slot, sections, section, leaving, states)
    return states.reshape(1, batches, batch_rows, depth)


def solution(mesh):
    in_specs = (
        P(None, "tensor", None),
        P("pipe", None),
        P("pipe", None, "tensor"),
        P("pipe", None, "tensor"),
        P("pipe", "tensor", None),
    )
    out_specs = P("pipe", None, "tensor", None)
    return jax.shard_map(local, mesh=mesh, in_specs=in_specs, out_specs=out_specs, check_vma=False)
```
